512 devices in a mesh: freq: 64 (over z_lo, x, core), lat: 8 (over z_hi, y).
Axes of the slice: x: 4, y: 4, z: 16 (z_hi: 2, z_lo: 8; z = z_hi * 8 + z_lo), core: 2. Of those that a mesh axis runs over, the one named last changes fastest.
Arguments:
- frequencies: float32 [64], P('freq'), may hold values from 0.3 to 1.5
- slowness: float32 [2, 128, 1024], P(None, 'lat', 'freq'), may hold values from 0.5 to 1.5
- src_field: float32 [64, 2, 128, 1024], P('freq', None, 'lat'), may hold values from -6 to 6
- rec_field: float32 [64, 2, 128, 1024], P('freq', None, 'lat'), may hold values from -6 to 6
Outputs:
- depth_image: float32 [2, 128, 1024], P(None, 'lat', 'freq')
- src_final: float32 [64, 2, 128, 1024], P('freq', None, 'lat')
- rec_final: float32 [64, 2, 128, 1024], P('freq', None, 'lat')
The draws below stay inside these ranges and needn't reach their ends.
All inputs are finite; a program needn't handle non-finite values.
Results may differ from the reference program's by a relative error of at most 0.0003.
Values sent between devices are 32-bit elements; how exact they have to be, the bound alone decides.
A program may use at most 64 MiB of HBM per device.

```python
import math
import jax
import jax.numpy as jnp
from jax import lax

NY = 1024
NZ = 2
TERMS = 8
NW = 64
NX = 128


def level_of(rng, shape, split, smallest, largest):
    gain = 1.0
    for axis_at, blocks in split:
        draws = jax.random.uniform(jax.random.fold_in(jax.random.fold_in(rng, 6), axis_at), (blocks,), jnp.float32, smallest / len(split), largest / len(split))
        gain = gain * jnp.repeat(jnp.exp(draws), shape[axis_at] // blocks).reshape((-1,) + (1,) * (len(shape) - 1 - axis_at))
    return gain


def centred(stream_key, extent, deviation, most, pieces=(), kind=jnp.bfloat16):
    factor_of = level_of(stream_key, extent, pieces, -0.22, 0.18) if pieces else 1.0
    values = jax.random.normal(stream_key, extent, jnp.float32) * deviation * factor_of
    return jnp.minimum(jnp.maximum(values, -most), most).astype(kind)


def setup_inputs(seed: int = 0) -> dict:
    splits = jax.random.split(jax.random.key(seed), 5)
    return {
        "frequencies": jnp.clip(jnp.exp(math.log(1.5) - 1.60943787 * jax.random.uniform(splits[0], (NW,), jnp.float32) ** level_of(splits[0], (NW,), ((0, 64),), -0.2, 0.2)), 0.3, 1.5),
        "slowness": jnp.clip(jnp.exp(math.log(1.5) - 1.0986123 * jax.random.uniform(splits[1], (NZ, NX, NY), jnp.float32) ** level_of(splits[1], (NZ, NX, NY), ((1, 8), (2, 64)), -0.2, 0.2)), 0.5, 1.5),
        "src_field": centred(splits[2], (NW, 2, NX, NY), 1.0, 6.0, ((0, 64), (2, 8)), jnp.float32),
        "rec_field": centred(splits[3], (NW, 2, NX, NY), 1.0, 6.0, ((0, 64), (2, 8)), jnp.float32),
    }


step_ratio = 1.0
damping = 0.1

def neighbours(values):
    zero_col = jnp.zeros_like(values[..., :1])
    from_right = jnp.concatenate([values[..., 1:], zero_col], axis=-1)
    from_left = jnp.concatenate([zero_col, values[..., :-1]], axis=-1)
    return from_right + from_left

def mcclellan(padded):
    centre = padded[..., 1:-1, :]
    vertical = padded[..., 2:, :] + padded[..., :-2, :]
    return -0.5 * centre + 0.25 * vertical + neighbours(0.25 * centre + 0.125 * vertical)

def coefficients(wavenum, term_count):
    angles = math.pi * (jnp.arange(term_count, dtype=jnp.float32) + 0.5) / term_count
    view_shape = (term_count,) + (1,) * wavenum.ndim
    node_angles = angles.reshape(view_shape)
    excess = wavenum[None] ** 2 - node_angles ** 2
    absorb = damping * wavenum[None] ** 2
    modulus = jnp.sqrt(excess * excess + absorb * absorb)
    larger = jnp.sqrt(0.5 * (modulus + jnp.abs(excess)))
    smaller = absorb / (2.0 * larger)
    propagating = excess >= 0
    real_part = jnp.where(propagating, larger, smaller)
    imag_part = jnp.where(propagating, smaller, larger)
    attenuation = jnp.exp(-step_ratio * imag_part)
    phase_re = attenuation * jnp.cos(step_ratio * real_part)
    phase_im = attenuation * jnp.sin(step_ratio * real_part)
    orders = jnp.arange(term_count, dtype=jnp.float32)
    weights = jnp.where(orders == 0, 1.0, 2.0) / term_count
    cosine_table = (weights[:, None] * jnp.cos(orders[:, None] * angles[None, :])).astype(jnp.float32)
    coef_re = jnp.einsum('nj,j...->n...', cosine_table, phase_re, precision=lax.Precision.HIGHEST)
    coef_im = jnp.einsum('nj,j...->n...', cosine_table, phase_im, precision=lax.Precision.HIGHEST)
    return (coef_re, coef_im)

def accumulate(summed, coef_re, coef_im, level):
    src_re = level[..., 0, :, :]
    src_im = level[..., 1, :, :]
    rec_re = level[..., 2, :, :]
    rec_im = level[..., 3, :, :]
    term = jnp.stack([coef_re * src_re - coef_im * src_im, coef_re * src_im + coef_im * src_re, coef_re * rec_re + coef_im * rec_im, coef_re * rec_im - coef_im * rec_re], axis=-3)
    return summed + term

def pad_rows(values):
    widths = [(0, 0)] * (values.ndim - 2) + [(1, 1), (0, 0)]
    return jnp.pad(values, widths)

def reference(frequencies, slowness, src_field, rec_field):

    def one_frequency(inputs):
        frequency, source, receiver = inputs
        wavefields = jnp.concatenate([source, receiver], axis=0)
        images = []
        for depth_step in range(NZ):
            coef_re, coef_im = coefficients(frequency * slowness[depth_step], TERMS)
            previous = wavefields
            summed = accumulate(jnp.zeros_like(wavefields), coef_re[0], coef_im[0], previous)
            current = mcclellan(pad_rows(previous))
            summed = accumulate(summed, coef_re[1], coef_im[1], current)
            for term_index in range(2, TERMS):
                following = 2.0 * mcclellan(pad_rows(current)) - previous
                summed = accumulate(summed, coef_re[term_index], coef_im[term_index], following)
                previous, current = (current, following)
            wavefields = summed
            images.append(wavefields[0] * wavefields[2] + wavefields[1] * wavefields[3])
        return (wavefields, jnp.stack(images))
    wavefields, images = lax.map(one_frequency, (frequencies, src_field, rec_field))
    depth_image = lax.optimization_barrier(jnp.sum(images, axis=0)) * (1.0 / math.sqrt(NW))
    return (depth_image, wavefields[:, :2], wavefields[:, 2:])
```

```python
import math

import jax
import jax.numpy as jnp
import numpy as np
from jax import lax
from jax.experimental import pallas as pl
from jax.experimental.pallas import tpu as pltpu
from jax.sharding import PartitionSpec as P

MESH = pl.DeviceIdType.MESH
LANES, GROUP = 128, 16
ROWS, TOP, END, HALO = 48, 16, 32, 14
PEERS = 32
LAT = 8

COSINE = [0.9999983310699463, -0.499983549118042, 0.041640717536211014, -0.0013744860189035535, 2.1503588868654333e-05]
SINC = [0.9999998211860657, -0.16666515171527863, 0.008330939337611198, -0.00019708606123458594, 2.452983835610212e-06]


def polynomial(terms, t):
    value = jnp.float32(terms[-1]) * t + jnp.float32(terms[-2])
    for term in terms[-3::-1]:
        value = value * t + jnp.float32(term)
    return value


def node_phases(wavenum):
    half = 0.5 * (wavenum * wavenum)
    absorb = 0.1 * half
    absorb2 = absorb * absorb
    parts = []
    for j in range(8):
        excess = half - jnp.float32(0.5 * (math.pi * (j + 0.5) / 8) ** 2)
        square = excess * excess + absorb2
        modulus = square * lax.rsqrt(square)
        total = modulus + jnp.abs(excess)
        inverse = lax.rsqrt(total)
        larger, smaller = total * inverse, absorb * inverse
        propagating = excess >= 0
        kr = jnp.where(propagating, larger, smaller)
        ki = jnp.where(propagating, smaller, larger)
        attenuation = jnp.exp2(ki * jnp.float32(-1.4426950408889634))
        t = kr * kr
        parts.append((attenuation * polynomial(COSINE, t), (attenuation * kr) * polynomial(SINC, t)))
    return parts


def cosine_sums(p):
    def c(n, j):
        return float(np.float32((1.0 if n == 0 else 2.0) / 8 * math.cos(n * math.pi * (j + 0.5) / 8)))

    even = [p[j] + p[7 - j] for j in range(4)]
    odd = [p[j] - p[7 - j] for j in range(4)]
    s0, s1, d0, d1 = even[0] + even[3], even[1] + even[2], even[0] - even[3], even[1] - even[2]
    h = [None] * 8
    h[0] = (s0 + s1) * c(0, 0)
    h[4] = (s0 - s1) * c(4, 0)
    h[2] = d0 * c(2, 0) + d1 * c(2, 1)
    h[6] = d0 * c(6, 0) + d1 * c(6, 1)
    for n in (1, 3, 5, 7):
        h[n] = (odd[0] * c(n, 0) + odd[1] * c(n, 1)) + (odd[2] * c(n, 2) + odd[3] * c(n, 3))
    return h


def at_row(row):
    return pl.ds(pl.multiple_of(row * 8, 8), 8)


def kernel(
    freq_ref, slow_ref, src_ref, rec_ref, img_ref, src_out, rec_out,
    stage, T, D, H, packed, gathered, slow, share, partner_share, summed, blocks,
    in_sem, out_sem, own_send, own_recv, edge_send, edge_recv, halo_send, halo_recv,
    core_send, core_recv, pair_send, pair_recv, part_send, part_recv,
):
    f, l = lax.axis_index("freq"), lax.axis_index("lat")
    core, place = f % 2, f // 2
    z, x = place // 4, place % 4
    partner = (f + 1 - 2 * core, l)

    def peer(k):
        return lax.rem(place + k, PEERS)

    lane = lax.broadcasted_iota(jnp.int32, (8, LANES), 1)
    sub = lax.broadcasted_iota(jnp.int32, (8, LANES), 0)
    group = lane // GROUP
    first, last = lane == 0, lane == LANES - 1
    corner = ((sub == 0) & first) | ((sub == 7) & last)
    diagonal = sub == group

    barrier = pltpu.get_barrier_semaphore()

    def greet(device):
        pl.semaphore_signal(barrier, inc=1, device_id=device, device_id_type=MESH)

    def greet_all(k, carry):
        to = peer(k) * 2 + core

        @pl.when(l < LAT - 1)
        def _():
            greet((to, l + 1))

        @pl.when(l > 0)
        def _():
            greet((to, l - 1))

        return carry

    lax.fori_loop(0, PEERS, greet_all, 0)

    def greet_own(k, carry):
        greet((peer(k) * 2 + core, l))
        return carry

    lax.fori_loop(1, PEERS, greet_own, 0)
    greet(partner)

    fetches = [
        pltpu.make_async_copy(ref.at[0], stage.at[pl.ds(2 * i, 2)], in_sem.at[i])
        for i, ref in enumerate((src_ref, rec_ref))
    ]
    for copy in fetches:
        copy.start()

    for layer in range(2):
        for half in range(2):
            block = jnp.concatenate(
                [slow_ref[layer, 8 * half : 8 * half + 8, :], jnp.zeros((8, LANES - GROUP), jnp.float32)], axis=1
            )
            for turn in (16, 32, 64):
                block = block + pltpu.roll(block, turn, 1)
            row = jnp.sum(jnp.where(diagonal, block, 0.0), axis=0, keepdims=True)
            packed[2 * layer + half : 2 * layer + half + 1, :] = row

    for i, copy in enumerate(fetches):
        copy.wait()
        for c in (2 * i, 2 * i + 1):
            for t in range(2):
                for j in range(8):
                    T[0, c, pl.ds((TOP + 8 * t) * 8 + j, 8, stride=8), :] = stage[
                        c, 8 * t : 8 * t + 8, LANES * j : LANES * j + LANES
                    ]

    pl.semaphore_wait(barrier, PEERS + PEERS * jnp.where((l == 0) | (l == LAT - 1), 1, 2))

    def own_copy(k):
        return pltpu.make_async_remote_copy(
            src_ref=packed.at[pl.ds(0, 4)],
            dst_ref=gathered.at[core, x, pl.ds(0, 4), z],
            send_sem=own_send.at[k], recv_sem=own_recv.at[k],
            device_id=(peer(k) * 2 + core, l), device_id_type=MESH,
        )

    def edge_copy(k, side):
        return pltpu.make_async_remote_copy(
            src_ref=packed.at[1 - side],
            dst_ref=gathered.at[core, x, 4 + side, z],
            send_sem=edge_send.at[side, k], recv_sem=edge_recv.at[side, k],
            device_id=(peer(k) * 2 + core, l + 1 - 2 * side), device_id_type=MESH,
        )

    def halo_copy(pair, side):
        return pltpu.make_async_remote_copy(
            src_ref=T.at[0, pl.ds(2 * pair, 2), pl.ds((END - HALO if side == 0 else TOP) * 8, HALO * 8)],
            dst_ref=T.at[0, pl.ds(2 * pair, 2), pl.ds((TOP - HALO if side == 0 else END) * 8, HALO * 8)],
            send_sem=halo_send.at[side, pair], recv_sem=halo_recv.at[side, pair],
            device_id=(f, l + 1 - 2 * side), device_id_type=MESH,
        )

    def each(count, start, do):
        def body(k, carry):
            do(k)
            return carry

        lax.fori_loop(start, count, body, 0)

    sends = [l < LAT - 1, l > 0]
    receives = [l > 0, l < LAT - 1]

    def own_start(k):
        own_copy(k).start()

    each(PEERS, 1, own_start)
    for side in range(2):

        @pl.when(sends[side])
        def _(side=side):
            each(PEERS, 0, lambda k: edge_copy(k, side).start())

    for pair in range(2):
        for side in range(2):

            @pl.when(sends[side])
            def _(side=side, pair=pair):
                halo_copy(pair, side).start()

    for m in range(4):
        gathered[core, x, m, pl.ds(z, 1), :] = packed[m : m + 1, :]

    inside = [jnp.broadcast_to(l > 0, (1, 8, LANES)), jnp.broadcast_to(l < LAT - 1, (1, 8, LANES))]

    def clear_edges():
        for side, row in ((0, TOP - 1), (1, END)):

            @pl.when(jnp.logical_not(receives[side]))
            def _(row=row):
                for c in range(4):
                    T[0, c, pl.ds(row * 8, 8), :] = jnp.zeros((8, LANES), jnp.float32)

    clear_edges()

    each(PEERS, 1, lambda k: own_copy(k).wait_recv())
    for side in range(2):

        @pl.when(receives[side])
        def _(side=side):
            each(PEERS, 0, lambda k: edge_copy(k, side).wait_recv())

    core_copy = pltpu.make_async_remote_copy(
        src_ref=gathered.at[core], dst_ref=gathered.at[core], send_sem=core_send, recv_sem=core_recv,
        device_id=partner, device_id_type=MESH,
    )
    core_copy.start()
    core_copy.wait_recv()

    def swap_groups(v):
        v = list(v)
        for bit in (1, 2, 4):
            low = (group // bit) % 2 == 0
            for a in range(8):
                if not a & bit:
                    lo, hi = v[a], v[a + bit]
                    v[a] = jnp.where(low, lo, pltpu.roll(hi, GROUP * bit, 1))
                    v[a + bit] = jnp.where(low, pltpu.roll(lo, LANES - GROUP * bit, 1), hi)
        return v

    for m, to in ((0, 8), (1, 16), (4, 0), (5, 24), (2, 32), (3, 40)):
        rows = swap_groups([gathered[j % 2, j // 2, m] for j in range(8)])
        for g in range(8):
            slow[(to + g) * 8 : (to + g) * 8 + 8, :] = rows[g]

    frequency = freq_ref[0]

    def coefficients(start, count, unroll):
        def body(i, carry):
            for u in range(unroll):
                r = start + i * unroll + u
                parts = node_phases(slow[at_row(r), :] * frequency)
                for which in range(2):
                    for n, value in enumerate(cosine_sums([p[which] for p in parts])):
                        H[at_row(r * 16 + which * 8 + n), :] = value
            return carry

        lax.fori_loop(0, count // unroll, body, 0)

    coefficients(1, 30, 5)
    coefficients(32, 16, 4)

    def raise_rows(n, c, lo, hi, edge):
        B = hi - lo
        rows = pl.ds(lo * 8, B * 8)
        v = T[n - 1, c, pl.ds((lo - 1) * 8, (B + 2) * 8), :].reshape(B + 2, 8, LANES)
        e = v[:-1] + v[1:]
        q = e[:-1] + e[1:]
        stopped = jnp.where(corner[None], 0.0, q)
        left = pltpu.roll(jnp.where(last[None], pltpu.roll(stopped, 1, 1), q), 1, 2)
        right = pltpu.roll(jnp.where(first[None], pltpu.roll(stopped, 7, 1), q), LANES - 1, 2)
        s = (left + right) + (q + q)
        d = 0.125 * s if n == 1 else 0.25 * s - D[c, rows, :].reshape(B, 8, LANES)
        D[c, rows, :] = d.reshape(B * 8, LANES)
        value = d - v[1:-1]
        if edge is not None:
            parts = [value[:-1], jnp.where(inside[0], value[-1:], 0.0)] if edge == 0 else [jnp.where(inside[1], value[:1], 0.0), value[1:]]
            value = jnp.concatenate([part for part in parts if part.shape[0]], axis=0)
        T[n, c, rows, :] = value.reshape(B * 8, LANES)

    def levels(reach, pair):
        for n in range(1, 8):
            out = reach - n
            for lo, hi, edge in ((TOP - out, TOP, 0), (TOP, TOP + 8, None), (TOP + 8, END, None), (END, END + out, 1)):
                if lo < hi:
                    for c in range(2):
                        raise_rows(n, 2 * pair + c, lo, hi, edge)

    def accumulate(start, lo, count, unroll):
        def body(i, carry):
            for u in range(unroll):
                r = i * unroll + u
                total = [None] * 4
                for n in range(8):
                    hr = H[at_row((start + r) * 16 + n), :]
                    hi = H[at_row((start + r) * 16 + 8 + n), :]
                    t = [T[n, c, at_row(lo + r), :] for c in range(4)]
                    term = [
                        hr * t[0] - hi * t[1],
                        hr * t[1] + hi * t[0],
                        hr * t[2] + hi * t[3],
                        hr * t[3] - hi * t[2],
                    ]
                    total = term if n == 0 else [a + b for a, b in zip(total, term)]
                for c in range(4):
                    T[0, c, at_row(lo + r), :] = total[c]
            return carry

        lax.fori_loop(0, count // unroll, body, 0)

    def pair_copy(layer):
        return pltpu.make_async_remote_copy(
            src_ref=share.at[layer, 1 - core], dst_ref=partner_share.at[layer],
            send_sem=pair_send.at[layer], recv_sem=pair_recv.at[layer],
            device_id=partner, device_id_type=MESH,
        )

    def part_copy(layer, k):
        to = peer(k)
        return pltpu.make_async_remote_copy(
            src_ref=summed.at[layer, to % 4, :, to // 4], dst_ref=blocks.at[layer, place],
            send_sem=part_send.at[layer, k], recv_sem=part_recv.at[layer, k],
            device_id=(to * 2 + core, l), device_id_type=MESH,
        )

    def image_terms(layer):
        for m in range(2):
            terms = []
            for g in range(8):
                s_re, s_im, r_re, r_im = (T[0, c, pl.ds((TOP + 8 * m + g) * 8, 8), :] for c in range(4))
                terms.append(s_re * r_re + s_im * r_im)
            for j, value in enumerate(swap_groups(terms)):
                share[layer, j % 2, j // 2, m] = value
        pair_copy(layer).start()

    def image_parts(layer):
        pair_copy(layer).wait_recv()
        summed[layer] = share[layer, core] + partner_share[layer]
        each(PEERS, 1, lambda k: part_copy(layer, k).start())
        for m in range(2):
            blocks[layer, place, m : m + 1, :] = summed[layer, x, m, pl.ds(z, 1), :]

    def image_sum(layer):
        each(PEERS, 1, lambda k: part_copy(layer, k).wait_recv())
        total = jnp.sum(blocks[layer], axis=0) * 0.125
        for m in range(2):
            row = jnp.where(diagonal, jnp.broadcast_to(total[m : m + 1, :], (8, LANES)), 0.0)
            for turn in (64, 32, 16):
                row = row + pltpu.roll(row, turn, 1)
            img_ref[layer, 8 * m : 8 * m + 8, :] = row[:, :GROUP]

    def first_levels(pair, carry):
        for side in range(2):

            @pl.when(receives[side])
            def _(side=side):
                halo_copy(pair, side).wait_recv()

        levels(HALO, pair)
        return carry

    lax.fori_loop(0, 2, first_levels, 0)
    for pair in range(2):
        for side in range(2):

            @pl.when(sends[side])
            def _(side=side, pair=pair):
                halo_copy(pair, side).wait_send()

    accumulate(1, TOP - 7, 30, 5)
    clear_edges()
    image_terms(0)

    levels(HALO // 2, 0)
    image_parts(0)
    levels(HALO // 2, 1)
    accumulate(32, TOP, 16, 4)
    image_terms(1)
    for c in range(4):
        for t in range(2):
            for j in range(8):
                stage[c, 8 * t : 8 * t + 8, LANES * j : LANES * j + LANES] = T[
                    0, c, pl.ds((TOP + 8 * t) * 8 + j, 8, stride=8), :
                ]
    stores = [
        pltpu.make_async_copy(stage.at[pl.ds(2 * i, 2)], ref.at[0], out_sem.at[i])
        for i, ref in enumerate((src_out, rec_out))
    ]
    image_parts(1)
    for copy in stores:
        copy.start()
    image_sum(0)
    each(PEERS, 1, lambda k: own_copy(k).wait_send())
    for side in range(2):

        @pl.when(sends[side])
        def _(side=side):
            each(PEERS, 0, lambda k: edge_copy(k, side).wait_send())

    core_copy.wait_send()
    for layer in range(2):
        pair_copy(layer).wait_send()
        each(PEERS, 1, lambda k: part_copy(layer, k).wait_send())
    for copy in stores:
        copy.wait()
    image_sum(1)


def migrate(frequencies, slowness, src_field, rec_field):
    f32 = jnp.float32
    field = jax.ShapeDtypeStruct(src_field.shape, f32)
    dma = pltpu.SemaphoreType.DMA
    return pl.pallas_call(
        kernel,
        out_shape=(jax.ShapeDtypeStruct(slowness.shape, f32), field, field),
        in_specs=[
            pl.BlockSpec(memory_space=pltpu.SMEM),
            pl.BlockSpec(memory_space=pltpu.VMEM),
            pl.BlockSpec(memory_space=pltpu.HBM),
            pl.BlockSpec(memory_space=pltpu.HBM),
        ],
        out_specs=(
            pl.BlockSpec(memory_space=pltpu.VMEM),
            pl.BlockSpec(memory_space=pl.ANY),
            pl.BlockSpec(memory_space=pl.ANY),
        ),
        scratch_shapes=[
            pltpu.VMEM((4, 16, 1024), f32),
            pltpu.VMEM((8, 4, ROWS * 8, LANES), f32),
            pltpu.VMEM((4, ROWS * 8, LANES), f32),
            pltpu.VMEM((48 * 16 * 8, LANES), f32),
            pltpu.VMEM((4, LANES), f32),
            pltpu.VMEM((2, 4, 6, 8, LANES), f32),
            pltpu.VMEM((48 * 8, LANES), f32),
            pltpu.VMEM((2, 2, 4, 2, 8, LANES), f32),
            pltpu.VMEM((2, 4, 2, 8, LANES), f32),
            pltpu.VMEM((2, 4, 2, 8, LANES), f32),
            pltpu.VMEM((2, PEERS, 2, LANES), f32),
            dma((2,)), dma((2,)),
            dma((PEERS,)), dma((PEERS,)),
            dma((2, PEERS)), dma((2, PEERS)),
            dma((2, 2)), dma((2, 2)),
            dma, dma,
            dma((2,)), dma((2,)),
            dma((2, PEERS)), dma((2, PEERS)),
        ],
        compiler_params=pltpu.CompilerParams(collective_id=0, has_side_effects=True, vmem_limit_bytes=40 << 20),
        name="migrate",
    )(frequencies, slowness, src_field, rec_field)


def solution(mesh):
    fields = P("freq", None, "lat", None)
    return jax.shard_map(
        migrate,
        mesh=mesh,
        in_specs=(P("freq"), P(None, "lat", "freq"), fields, fields),
        out_specs=(P(None, "lat", "freq"), fields, fields),
        check_vma=False,
    )
```

```python
import math

import jax
import jax.numpy as jnp
import numpy as np
from jax import lax
from jax.experimental import pallas as pl
from jax.experimental.pallas import tpu as pltpu
from jax.sharding import PartitionSpec as P

MESH = pl.DeviceIdType.MESH
LANES, GROUP = 128, 16
ROWS, TOP, END, HALO = 48, 16, 32, 14
PEERS = 32
LAT = 8

COSINE = [0.9999983310699463, -0.499983549118042, 0.041640717536211014, -0.0013744860189035535, 2.1503588868654333e-05]
SINC = [0.9999998211860657, -0.16666515171527863, 0.008330939337611198, -0.00019708606123458594, 2.452983835610212e-06]


def polynomial(terms, t):
    value = jnp.float32(terms[-1]) * t + jnp.float32(terms[-2])
    for term in terms[-3::-1]:
        value = value * t + jnp.float32(term)
    return value


def node_phases(wavenum):
    half = 0.5 * (wavenum * wavenum)
    absorb = 0.1 * half
    absorb2 = absorb * absorb
    parts = []
    for j in range(8):
        excess = half - jnp.float32(0.5 * (math.pi * (j + 0.5) / 8) ** 2)
        square = excess * excess + absorb2
        modulus = square * lax.rsqrt(square)
        total = modulus + jnp.abs(excess)
        inverse = lax.rsqrt(total)
        larger, smaller = total * inverse, absorb * inverse
        propagating = excess >= 0
        kr = jnp.where(propagating, larger, smaller)
        ki = jnp.where(propagating, smaller, larger)
        attenuation = jnp.exp2(ki * jnp.float32(-1.4426950408889634))
        t = kr * kr
        parts.append((attenuation * polynomial(COSINE, t), (attenuation * kr) * polynomial(SINC, t)))
    return parts


def cosine_sums(p):
    def c(n, j):
        return float(np.float32((1.0 if n == 0 else 2.0) / 8 * math.cos(n * math.pi * (j + 0.5) / 8)))

    even = [p[j] + p[7 - j] for j in range(4)]
    odd = [p[j] - p[7 - j] for j in range(4)]
    s0, s1, d0, d1 = even[0] + even[3], even[1] + even[2], even[0] - even[3], even[1] - even[2]
    h = [None] * 8
    h[0] = (s0 + s1) * c(0, 0)
    h[4] = (s0 - s1) * c(4, 0)
    h[2] = d0 * c(2, 0) + d1 * c(2, 1)
    h[6] = d0 * c(6, 0) + d1 * c(6, 1)
    for n in (1, 3, 5, 7):
        h[n] = (odd[0] * c(n, 0) + odd[1] * c(n, 1)) + (odd[2] * c(n, 2) + odd[3] * c(n, 3))
    return h


def at_row(row):
    return pl.ds(pl.multiple_of(row * 8, 8), 8)


def kernel(
    freq_hbm, slow_hbm, src_ref, rec_ref, img_ref, src_out, rec_out,
    freq_ref, slow_ref, stage, T, D, H, packed, gathered, slow, relay, share, partner_share, summed, blocks,
    in_sem, out_sem, own_send, own_recv, edge_send, edge_recv, halo_send, halo_recv, relay_send, relay_recv,
    core_send, core_recv, pair_send, pair_recv, part_send, part_recv,
):
    f, l = lax.axis_index("freq"), lax.axis_index("lat")
    core, place = f % 2, f // 2
    z, x = place // 4, place % 4
    partner = (f + 1 - 2 * core, l)

    def peer(k):
        return lax.rem(place + k, PEERS)

    lane = lax.broadcasted_iota(jnp.int32, (8, LANES), 1)
    sub = lax.broadcasted_iota(jnp.int32, (8, LANES), 0)
    group = lane // GROUP
    first, last = lane == 0, lane == LANES - 1
    corner = ((sub == 0) & first) | ((sub == 7) & last)
    diagonal = sub == group

    fetches = [
        pltpu.make_async_copy(ref.at[0], stage.at[pl.ds(2 * i, 2)], in_sem.at[i])
        for i, ref in enumerate((src_ref, rec_ref))
    ]
    fetch_slow = pltpu.make_async_copy(slow_hbm, slow_ref, in_sem.at[2])
    fetch_freq = pltpu.make_async_copy(freq_hbm, freq_ref, in_sem.at[3])
    for copy in (fetch_slow, *fetches, fetch_freq):
        copy.start()

    barrier = pltpu.get_barrier_semaphore()

    def greet(device):
        pl.semaphore_signal(barrier, inc=1, device_id=device, device_id_type=MESH)

    for k in range(PEERS - 1, -1, -1):
        to = peer(k) * 2 + core

        @pl.when(l < LAT - 1)
        def _(to=to):
            greet((to, l + 1))

        @pl.when(l > 0)
        def _(to=to):
            greet((to, l - 1))

    for k in range(PEERS - 1, 0, -1):
        greet((peer(k) * 2 + core, l))
    for k in range(2, LAT - 1):
        away = lax.rem(l + k, LAT)

        @pl.when((away - l) * (away - l) > 1)
        def _(away=away):
            greet((f, away))

    for k in (1, LAT - 1):
        away = lax.rem(l + k, LAT)

        @pl.when((away - l) * (away - l) > 1)
        def _(away=away):
            greet((f, away))

    greet(partner)

    fetch_slow.wait()

    for layer in range(2):
        for half in range(2):
            block = jnp.concatenate(
                [slow_ref[layer, 8 * half : 8 * half + 8, :], jnp.zeros((8, LANES - GROUP), jnp.float32)], axis=1
            )
            for turn in (16, 32, 64):
                block = block + pltpu.roll(block, turn, 1)
            row = jnp.sum(jnp.where(diagonal, block, 0.0), axis=0, keepdims=True)
            packed[2 * layer + half : 2 * layer + half + 1, :] = row

    for i, copy in enumerate(fetches):
        copy.wait()
        for c in (2 * i, 2 * i + 1):
            for t in range(2):
                for j in range(8):
                    T[0, c, pl.ds((TOP + 8 * t) * 8 + j, 8, stride=8), :] = stage[
                        c, 8 * t : 8 * t + 8, LANES * j : LANES * j + LANES
                    ]

    pl.semaphore_wait(barrier, PEERS + jnp.where((l == 0) | (l == LAT - 1), PEERS + LAT - 2, 2 * PEERS + LAT - 3))

    def own_copy(k):
        return pltpu.make_async_remote_copy(
            src_ref=packed.at[pl.ds(0, 4)],
            dst_ref=gathered.at[core, x, pl.ds(0, 4), z],
            send_sem=own_send, recv_sem=own_recv,
            device_id=(peer(k) * 2 + core, l), device_id_type=MESH,
        )

    def edge_copy(k, side):
        return pltpu.make_async_remote_copy(
            src_ref=packed.at[1 - side],
            dst_ref=gathered.at[core, x, 4 + side, z],
            send_sem=edge_send.at[side], recv_sem=edge_recv.at[side],
            device_id=(peer(k) * 2 + core, l + 1 - 2 * side), device_id_type=MESH,
        )

    def halo_rows(side):
        down = side == 0
        return (END - HALO, TOP - HALO) if down else (TOP, END)

    def halo_copy(c, side):
        read, land = halo_rows(side)
        return pltpu.make_async_remote_copy(
            src_ref=T.at[0, c, pl.ds(read * 8, HALO * 8)],
            dst_ref=T.at[0, c, pl.ds(land * 8, HALO * 8)],
            send_sem=halo_send.at[side, c], recv_sem=halo_recv.at[side, c],
            device_id=(f, l + 1 - 2 * side), device_id_type=MESH,
        )

    lower = l < LAT // 2
    step = jnp.where(lower, l, LAT - 1 - l)
    across = jnp.where(lower, LAT // 2, LAT // 2 - 1)

    def to_relay(c, side):
        read, _ = halo_rows(side)
        return pltpu.make_async_remote_copy(
            src_ref=T.at[0, c, pl.ds(read * 8, HALO * 8)], dst_ref=relay,
            send_sem=relay_send.at[c], recv_sem=relay_recv.at[0],
            device_id=(f, c if side == 0 else LAT - 1 - c), device_id_type=MESH,
        )

    def from_relay(c, side):
        _, land = halo_rows(side)
        return pltpu.make_async_remote_copy(
            src_ref=relay, dst_ref=T.at[0, c, pl.ds(land * 8, HALO * 8)],
            send_sem=relay_send.at[3], recv_sem=halo_recv.at[side, c],
            device_id=(f, across), device_id_type=MESH,
        )

    def bytes_of(rows, sem):
        return pltpu.make_async_copy(H.at[pl.ds(0, rows)], H.at[pl.ds(0, rows)], sem)

    sends = [l < LAT - 1, l > 0]
    receives = [l > 0, l < LAT - 1]

    middle = [l == LAT // 2 - 1, l == LAT // 2]
    for side in range(2):

        @pl.when(middle[side])
        def _(side=side):
            for c in range(3):
                to_relay(c, side).start()
            halo_copy(3, side).start()

    for k in range(PEERS - 1, 0, -1):
        own_copy(k).start()
    for side in range(2):

        @pl.when(sends[side])
        def _(side=side):
            for k in range(PEERS - 1, -1, -1):
                edge_copy(k, side).start()

    for side in range(2):

        @pl.when(sends[side] & jnp.logical_not(middle[side]))
        def _(side=side):
            for c in range(4):
                halo_copy(c, side).start()

    for m in range(4):
        gathered[core, x, m, pl.ds(z, 1), :] = packed[m : m + 1, :]

    inside = [jnp.broadcast_to(l > 0, (1, 8, LANES)), jnp.broadcast_to(l < LAT - 1, (1, 8, LANES))]

    def clear_edges():
        for side, row in ((0, TOP - 1), (1, END)):

            @pl.when(jnp.logical_not(receives[side]))
            def _(row=row):
                for c in range(4):
                    T[0, c, pl.ds(row * 8, 8), :] = jnp.zeros((8, LANES), jnp.float32)

    clear_edges()

    for c in range(3):
        for side in range(2):

            @pl.when((step == c) & (lower if side == 0 else jnp.logical_not(lower)))
            def _(c=c, side=side):
                to_relay(c, side).wait_recv()
                from_relay(c, side).start()

    bytes_of(4 * (PEERS - 1), own_recv).wait()
    for side in range(2):

        @pl.when(receives[side])
        def _(side=side):
            bytes_of(PEERS, edge_recv.at[side]).wait()

    core_copy = pltpu.make_async_remote_copy(
        src_ref=gathered.at[core], dst_ref=gathered.at[core], send_sem=core_send, recv_sem=core_recv,
        device_id=partner, device_id_type=MESH,
    )
    core_copy.start()
    core_copy.wait_recv()

    def swap_groups(v):
        v = list(v)
        for bit in (1, 2, 4):
            low = (group // bit) % 2 == 0
            for a in range(8):
                if not a & bit:
                    lo, hi = v[a], v[a + bit]
                    v[a] = jnp.where(low, lo, pltpu.roll(hi, GROUP * bit, 1))
                    v[a + bit] = jnp.where(low, pltpu.roll(lo, LANES - GROUP * bit, 1), hi)
        return v

    for m, to in ((0, 8), (1, 16), (4, 0), (5, 24), (2, 32), (3, 40)):
        rows = swap_groups([gathered[j % 2, j // 2, m] for j in range(8)])
        for g in range(8):
            slow[(to + g) * 8 : (to + g) * 8 + 8, :] = rows[g]

    fetch_freq.wait()
    frequency = freq_ref[0]

    def coefficients(start, count, unroll):
        def body(i, carry):
            for u in range(unroll):
                r = start + i * unroll + u
                parts = node_phases(slow[at_row(r), :] * frequency)
                for which in range(2):
                    for n, value in enumerate(cosine_sums([p[which] for p in parts])):
                        H[at_row(r * 16 + which * 8 + n), :] = value
            return carry

        lax.fori_loop(0, count // unroll, body, 0)

    coefficients(1, 30, 5)
    coefficients(32, 16, 4)

    def raise_rows(n, c, lo, hi, edge):
        B = hi - lo
        rows = pl.ds(lo * 8, B * 8)
        v = T[n - 1, c, pl.ds((lo - 1) * 8, (B + 2) * 8), :].reshape(B + 2, 8, LANES)
        e = v[:-1] + v[1:]
        q = e[:-1] + e[1:]
        stopped = jnp.where(corner[None], 0.0, q)
        left = pltpu.roll(jnp.where(last[None], pltpu.roll(stopped, 1, 1), q), 1, 2)
        right = pltpu.roll(jnp.where(first[None], pltpu.roll(stopped, 7, 1), q), LANES - 1, 2)
        s = (left + right) + (q + q)
        d = 0.125 * s if n == 1 else 0.25 * s - D[c, rows, :].reshape(B, 8, LANES)
        D[c, rows, :] = d.reshape(B * 8, LANES)
        value = d - v[1:-1]
        if edge is not None:
            parts = [value[:-1], jnp.where(inside[0], value[-1:], 0.0)] if edge == 0 else [jnp.where(inside[1], value[:1], 0.0), value[1:]]
            value = jnp.concatenate([part for part in parts if part.shape[0]], axis=0)
        T[n, c, rows, :] = value.reshape(B * 8, LANES)

    def levels(reach, pair):
        for n in range(1, 8):
            out = reach - n
            for lo, hi, edge in ((TOP - out, TOP, 0), (TOP, TOP + 8, None), (TOP + 8, END, None), (END, END + out, 1)):
                if lo < hi:
                    for c in range(2):
                        raise_rows(n, 2 * pair + c, lo, hi, edge)

    def accumulate(start, lo, count, unroll):
        def body(i, carry):
            for u in range(unroll):
                r = i * unroll + u
                total = [None] * 4
                for n in range(8):
                    hr = H[at_row((start + r) * 16 + n), :]
                    hi = H[at_row((start + r) * 16 + 8 + n), :]
                    t = [T[n, c, at_row(lo + r), :] for c in range(4)]
                    term = [
                        hr * t[0] - hi * t[1],
                        hr * t[1] + hi * t[0],
                        hr * t[2] + hi * t[3],
                        hr * t[3] - hi * t[2],
                    ]
                    total = term if n == 0 else [a + b for a, b in zip(total, term)]
                for c in range(4):
                    T[0, c, at_row(lo + r), :] = total[c]
            return carry

        lax.fori_loop(0, count // unroll, body, 0)

    def pair_copy(layer):
        return pltpu.make_async_remote_copy(
            src_ref=share.at[layer, 1 - core], dst_ref=partner_share.at[layer],
            send_sem=pair_send.at[layer], recv_sem=pair_recv.at[layer],
            device_id=partner, device_id_type=MESH,
        )

    def part_copy(layer, k):
        to = peer(k)
        return pltpu.make_async_remote_copy(
            src_ref=summed.at[layer, to % 4, :, to // 4], dst_ref=blocks.at[layer, place],
            send_sem=part_send.at[layer], recv_sem=part_recv.at[layer],
            device_id=(to * 2 + core, l), device_id_type=MESH,
        )

    def image_terms(layer):
        for m in range(2):
            terms = []
            for g in range(8):
                s_re, s_im, r_re, r_im = (T[0, c, pl.ds((TOP + 8 * m + g) * 8, 8), :] for c in range(4))
                terms.append(s_re * r_re + s_im * r_im)
            for j, value in enumerate(swap_groups(terms)):
                share[layer, j % 2, j // 2, m] = value
        pair_copy(layer).start()

    def image_parts(layer):
        pair_copy(layer).wait_recv()
        summed[layer] = share[layer, core] + partner_share[layer]
        for k in range(PEERS - 1, 0, -1):
            part_copy(layer, k).start()
        for m in range(2):
            blocks[layer, place, m : m + 1, :] = summed[layer, x, m, pl.ds(z, 1), :]

    def image_sum(layer):
        bytes_of(2 * (PEERS - 1), part_recv.at[layer]).wait()
        total = jnp.sum(blocks[layer], axis=0) * 0.125
        for m in range(2):
            row = jnp.where(diagonal, jnp.broadcast_to(total[m : m + 1, :], (8, LANES)), 0.0)
            for turn in (64, 32, 16):
                row = row + pltpu.roll(row, turn, 1)
            img_ref[layer, 8 * m : 8 * m + 8, :] = row[:, :GROUP]

    def first_levels(pair, carry):
        for side in range(2):

            @pl.when(receives[side])
            def _(side=side):
                for c in range(2):
                    halo_copy(2 * pair + c, side).wait_recv()

        levels(HALO, pair)
        return carry

    lax.fori_loop(0, 2, first_levels, 0)
    for side in range(2):

        @pl.when(sends[side] & jnp.logical_not(middle[side]))
        def _(side=side):
            for c in range(4):
                halo_copy(c, side).wait_send()

        @pl.when(middle[side])
        def _(side=side):
            for c in range(3):
                to_relay(c, side).wait_send()
            halo_copy(3, side).wait_send()

    @pl.when(step < 3)
    def _():
        from_relay(0, 0).wait_send()

    accumulate(1, TOP - 7, 30, 5)
    clear_edges()
    image_terms(0)

    levels(HALO // 2, 0)
    image_parts(0)
    levels(HALO // 2, 1)
    accumulate(32, TOP, 16, 4)
    image_terms(1)
    for c in range(4):
        for t in range(2):
            for j in range(8):
                stage[c, 8 * t : 8 * t + 8, LANES * j : LANES * j + LANES] = T[
                    0, c, pl.ds((TOP + 8 * t) * 8 + j, 8, stride=8), :
                ]
    stores = [
        pltpu.make_async_copy(stage.at[pl.ds(2 * i, 2)], ref.at[0], out_sem.at[i])
        for i, ref in enumerate((src_out, rec_out))
    ]
    image_parts(1)
    for copy in stores:
        copy.start()
    image_sum(0)
    bytes_of(4 * (PEERS - 1), own_send).wait()
    for side in range(2):

        @pl.when(sends[side])
        def _(side=side):
            bytes_of(PEERS, edge_send.at[side]).wait()

    core_copy.wait_send()
    for layer in range(2):
        pair_copy(layer).wait_send()
        bytes_of(2 * (PEERS - 1), part_send.at[layer]).wait()
    for copy in stores:
        copy.wait()
    image_sum(1)


def migrate(frequencies, slowness, src_field, rec_field):
    f32 = jnp.float32
    field = jax.ShapeDtypeStruct(src_field.shape, f32)
    dma = pltpu.SemaphoreType.DMA
    return pl.pallas_call(
        kernel,
        out_shape=(jax.ShapeDtypeStruct(slowness.shape, f32), field, field),
        in_specs=[
            pl.BlockSpec(memory_space=pltpu.HBM),
            pl.BlockSpec(memory_space=pltpu.HBM),
            pl.BlockSpec(memory_space=pltpu.HBM),
            pl.BlockSpec(memory_space=pltpu.HBM),
        ],
        out_specs=(
            pl.BlockSpec(memory_space=pltpu.VMEM),
            pl.BlockSpec(memory_space=pl.ANY),
            pl.BlockSpec(memory_space=pl.ANY),
        ),
        scratch_shapes=[
            pltpu.SMEM((1,), f32),
            pltpu.VMEM((2, 16, 16), f32),
            pltpu.VMEM((4, 16, 1024), f32),
            pltpu.VMEM((8, 4, ROWS * 8, LANES), f32),
            pltpu.VMEM((4, ROWS * 8, LANES), f32),
            pltpu.VMEM((48 * 16 * 8, LANES), f32),
            pltpu.VMEM((4, LANES), f32),
            pltpu.VMEM((2, 4, 6, 8, LANES), f32),
            pltpu.VMEM((48 * 8, LANES), f32),
            pltpu.VMEM((HALO * 8, LANES), f32),
            pltpu.VMEM((2, 2, 4, 2, 8, LANES), f32),
            pltpu.VMEM((2, 4, 2, 8, LANES), f32),
            pltpu.VMEM((2, 4, 2, 8, LANES), f32),
            pltpu.VMEM((2, PEERS, 2, LANES), f32),
            dma((4,)), dma((2,)),
            dma, dma,
            dma((2,)), dma((2,)),
            dma((2, 4)), dma((2, 4)),
            dma((4,)), dma((4,)),
            dma, dma,
            dma((2,)), dma((2,)),
            dma((2,)), dma((2,)),
        ],
        compiler_params=pltpu.CompilerParams(collective_id=0, has_side_effects=True, vmem_limit_bytes=64 << 20),
        name="migrate",
    )(frequencies, slowness, src_field, rec_field)


def solution(mesh):
    fields = P("freq", None, "lat", None)
    return jax.shard_map(
        migrate,
        mesh=mesh,
        in_specs=(P("freq"), P(None, "lat", "freq"), fields, fields),
        out_specs=(P(None, "lat", "freq"), fields, fields),
        check_vma=False,
    )
```

```python
import math

import jax
import jax.numpy as jnp
import numpy as np
from jax import lax
from jax.experimental import pallas as pl
from jax.experimental.pallas import tpu as pltpu
from jax.sharding import PartitionSpec as P

MESH = pl.DeviceIdType.MESH
LANES, GROUP = 128, 16
ROWS, TOP, END, HALO = 48, 16, 32, 14
PEERS = 32
LAT = 8

COSINE = [0.9999983310699463, -0.499983549118042, 0.041640717536211014, -0.0013744860189035535, 2.1503588868654333e-05]
SINC = [0.9999998211860657, -0.16666515171527863, 0.008330939337611198, -0.00019708606123458594, 2.452983835610212e-06]


def polynomial(terms, t):
    value = jnp.float32(terms[-1]) * t + jnp.float32(terms[-2])
    for term in terms[-3::-1]:
        value = value * t + jnp.float32(term)
    return value


def node_phases(wavenum):
    half = 0.5 * (wavenum * wavenum)
    absorb = 0.1 * half
    absorb2 = absorb * absorb
    parts = []
    for j in range(8):
        excess = half - jnp.float32(0.5 * (math.pi * (j + 0.5) / 8) ** 2)
        square = excess * excess + absorb2
        modulus = square * lax.rsqrt(square)
        total = modulus + jnp.abs(excess)
        inverse = lax.rsqrt(total)
        larger, smaller = total * inverse, absorb * inverse
        propagating = excess >= 0
        kr = jnp.where(propagating, larger, smaller)
        ki = jnp.where(propagating, smaller, larger)
        attenuation = jnp.exp2(ki * jnp.float32(-1.4426950408889634))
        t = kr * kr
        parts.append((attenuation * polynomial(COSINE, t), (attenuation * kr) * polynomial(SINC, t)))
    return parts


def cosine_sums(p):
    def c(n, j):
        return float(np.float32((1.0 if n == 0 else 2.0) / 8 * math.cos(n * math.pi * (j + 0.5) / 8)))

    even = [p[j] + p[7 - j] for j in range(4)]
    odd = [p[j] - p[7 - j] for j in range(4)]
    s0, s1, d0, d1 = even[0] + even[3], even[1] + even[2], even[0] - even[3], even[1] - even[2]
    h = [None] * 8
    h[0] = (s0 + s1) * c(0, 0)
    h[4] = (s0 - s1) * c(4, 0)
    h[2] = d0 * c(2, 0) + d1 * c(2, 1)
    h[6] = d0 * c(6, 0) + d1 * c(6, 1)
    for n in (1, 3, 5, 7):
        h[n] = (odd[0] * c(n, 0) + odd[1] * c(n, 1)) + (odd[2] * c(n, 2) + odd[3] * c(n, 3))
    return h


def at_row(row):
    return pl.ds(pl.multiple_of(row * 8, 8), 8)


def kernel(
    freq_hbm, slow_hbm, src_ref, rec_ref, img_ref, src_out, rec_out,
    freq_ref, slow_ref, stage, T, D, H, packed, gathered, slow, relay, share, partner_share, summed, blocks,
    in_sem, out_sem, own_send, own_recv, edge_send, edge_recv, halo_send, halo_recv, relay_send, relay_recv,
    core_send, core_recv, pair_send, pair_recv, part_send, part_recv,
):
    f, l = lax.axis_index("freq"), lax.axis_index("lat")
    core, place = f % 2, f // 2
    z, x = place // 4, place % 4
    partner = (f + 1 - 2 * core, l)

    def peer(k):
        return lax.rem(place + k, PEERS)

    lane = lax.broadcasted_iota(jnp.int32, (8, LANES), 1)
    sub = lax.broadcasted_iota(jnp.int32, (8, LANES), 0)
    group = lane // GROUP
    first, last = lane == 0, lane == LANES - 1
    corner = ((sub == 0) & first) | ((sub == 7) & last)
    diagonal = sub == group

    fetches = [
        pltpu.make_async_copy(ref.at[0], stage.at[pl.ds(2 * i, 2)], in_sem.at[i])
        for i, ref in enumerate((src_ref, rec_ref))
    ]
    fetch_slow = pltpu.make_async_copy(slow_hbm, slow_ref, in_sem.at[2])
    fetch_freq = pltpu.make_async_copy(freq_hbm, freq_ref, in_sem.at[3])
    for copy in (fetch_slow, *fetches, fetch_freq):
        copy.start()

    barrier = pltpu.get_barrier_semaphore()

    def greet(device):
        pl.semaphore_signal(barrier, inc=1, device_id=device, device_id_type=MESH)

    for to in range(PEERS):

        @pl.when(to != place)
        def _(to=to):
            greet((to * 2 + core, l))

    for to in range(PEERS):

        @pl.when(l < LAT - 1)
        def _(to=to):
            greet((to * 2 + core, l + 1))

        @pl.when(l > 0)
        def _(to=to):
            greet((to * 2 + core, l - 1))

    for one, other in ((3, 0), (3, 1), (4, 0), (4, 1), (4, 2), (3, 5), (3, 6), (3, 7), (4, 6), (4, 7)):
        for here, there in ((one, other), (other, one)):

            @pl.when(l == here)
            def _(there=there):
                greet((f, there))

    greet(partner)

    fetch_slow.wait()

    for layer in range(2):
        for half in range(2):
            block = jnp.concatenate(
                [slow_ref[layer, 8 * half : 8 * half + 8, :], jnp.zeros((8, LANES - GROUP), jnp.float32)], axis=1
            )
            for turn in (16, 32, 64):
                block = block + pltpu.roll(block, turn, 1)
            row = jnp.sum(jnp.where(diagonal, block, 0.0), axis=0, keepdims=True)
            packed[2 * layer + half : 2 * layer + half + 1, :] = row

    for i, copy in enumerate(fetches):
        copy.wait()
        for c in (2 * i, 2 * i + 1):
            for t in range(2):
                for j in range(8):
                    T[0, c, pl.ds((TOP + 8 * t) * 8 + j, 8, stride=8), :] = stage[
                        c, 8 * t : 8 * t + 8, LANES * j : LANES * j + LANES
                    ]

    relays = jnp.where((l == 3) | (l == 4), 5, jnp.where((l == 2) | (l == 5), 1, 2))
    pl.semaphore_wait(barrier, PEERS + PEERS * jnp.where((l == 0) | (l == LAT - 1), 1, 2) + relays)

    def own_copy(k):
        return pltpu.make_async_remote_copy(
            src_ref=packed.at[pl.ds(0, 4)],
            dst_ref=gathered.at[core, x, pl.ds(0, 4), z],
            send_sem=own_send, recv_sem=own_recv,
            device_id=(peer(k) * 2 + core, l), device_id_type=MESH,
        )

    def edge_copy(k, side):
        return pltpu.make_async_remote_copy(
            src_ref=packed.at[1 - side],
            dst_ref=gathered.at[core, x, 4 + side, z],
            send_sem=edge_send.at[side], recv_sem=edge_recv.at[side],
            device_id=(peer(k) * 2 + core, l + 1 - 2 * side), device_id_type=MESH,
        )

    def halo_rows(side):
        down = side == 0
        return (END - HALO, TOP - HALO) if down else (TOP, END)

    def halo_copy(c, side):
        read, land = halo_rows(side)
        return pltpu.make_async_remote_copy(
            src_ref=T.at[0, c, pl.ds(read * 8, HALO * 8)],
            dst_ref=T.at[0, c, pl.ds(land * 8, HALO * 8)],
            send_sem=halo_send.at[side, c], recv_sem=halo_recv.at[side, c],
            device_id=(f, l + 1 - 2 * side), device_id_type=MESH,
        )

    def to_relay(c, side):
        read, _ = halo_rows(side)
        return pltpu.make_async_remote_copy(
            src_ref=T.at[0, c, pl.ds(read * 8, HALO * 8)], dst_ref=relay,
            send_sem=halo_send.at[side, c], recv_sem=relay_recv,
            device_id=(f, c if side == 0 else LAT - 1 - c), device_id_type=MESH,
        )

    def from_relay(c, side):
        _, land = halo_rows(side)
        return pltpu.make_async_remote_copy(
            src_ref=relay, dst_ref=T.at[0, c, pl.ds(land * 8, HALO * 8)],
            send_sem=relay_send, recv_sem=halo_recv.at[side, c],
            device_id=(f, LAT // 2 - side), device_id_type=MESH,
        )

    def bytes_of(rows, sem):
        return pltpu.make_async_copy(H.at[pl.ds(0, rows)], H.at[pl.ds(0, rows)], sem)

    sends = [l < LAT - 1, l > 0]
    receives = [l > 0, l < LAT - 1]

    middle = [l == LAT // 2 - 1, l == LAT // 2]
    for side in range(2):

        @pl.when(middle[side])
        def _(side=side):
            for c in range(3):
                to_relay(c, side).start()
            halo_copy(3, side).start()

    for k in range(PEERS - 1, 0, -1):
        own_copy(k).start()
    for side in range(2):

        @pl.when(sends[side])
        def _(side=side):
            for k in range(PEERS - 1, -1, -1):
                edge_copy(k, side).start()

    for side in range(2):

        @pl.when(sends[side] & jnp.logical_not(middle[side]))
        def _(side=side):
            for c in range(4):
                halo_copy(c, side).start()

    for m in range(4):
        gathered[core, x, m, pl.ds(z, 1), :] = packed[m : m + 1, :]

    inside = [jnp.broadcast_to(l > 0, (1, 8, LANES)), jnp.broadcast_to(l < LAT - 1, (1, 8, LANES))]

    def clear_edges():
        for side, row in ((0, TOP - 1), (1, END)):

            @pl.when(jnp.logical_not(receives[side]))
            def _(row=row):
                for c in range(4):
                    T[0, c, pl.ds(row * 8, 8), :] = jnp.zeros((8, LANES), jnp.float32)

    clear_edges()

    def pass_on(side):
        for c in range(3):

            @pl.when(l == (c if side == 0 else LAT - 1 - c))
            def _(c=c):
                to_relay(c, side).wait_recv()
                from_relay(c, side).start()

    pass_on(1)

    def raise_rows(n, c, lo, hi, edge):
        B = hi - lo
        rows = pl.ds(lo * 8, B * 8)
        v = T[n - 1, c, pl.ds((lo - 1) * 8, (B + 2) * 8), :].reshape(B + 2, 8, LANES)
        e = v[:-1] + v[1:]
        q = e[:-1] + e[1:]
        stopped = jnp.where(corner[None], 0.0, q)
        left = pltpu.roll(jnp.where(last[None], pltpu.roll(stopped, 1, 1), q), 1, 2)
        right = pltpu.roll(jnp.where(first[None], pltpu.roll(stopped, 7, 1), q), LANES - 1, 2)
        s = (left + right) + (q + q)
        d = 0.125 * s if n == 1 else 0.25 * s - D[c, rows, :].reshape(B, 8, LANES)
        D[c, rows, :] = d.reshape(B * 8, LANES)
        value = d - v[1:-1]
        if edge is not None:
            parts = [value[:-1], jnp.where(inside[0], value[-1:], 0.0)] if edge == 0 else [jnp.where(inside[1], value[:1], 0.0), value[1:]]
            value = jnp.concatenate([part for part in parts if part.shape[0]], axis=0)
        T[n, c, rows, :] = value.reshape(B * 8, LANES)

    def levels(reach, pair):
        for n in range(1, 8):
            out = reach - n
            for lo, hi, edge in ((TOP - out, TOP, 0), (TOP, TOP + 8, None), (TOP + 8, END, None), (END, END + out, 1)):
                if lo < hi:
                    for c in range(2):
                        raise_rows(n, 2 * pair + c, lo, hi, edge)

    def first_levels(pair, carry):
        for side in range(2):

            @pl.when(receives[side])
            def _(side=side):
                for c in range(2):
                    halo_copy(2 * pair + c, side).wait_recv()

        levels(HALO, pair)
        return carry

    crossing = middle[0] | middle[1]

    @pl.when(jnp.logical_not(crossing))
    def _():
        lax.fori_loop(0, 2, first_levels, 0)

    bytes_of(4 * (PEERS - 1), own_recv).wait()
    for side in range(2):

        @pl.when(receives[side])
        def _(side=side):
            bytes_of(PEERS, edge_recv.at[side]).wait()

    core_copy = pltpu.make_async_remote_copy(
        src_ref=gathered.at[core], dst_ref=gathered.at[core], send_sem=core_send, recv_sem=core_recv,
        device_id=partner, device_id_type=MESH,
    )
    core_copy.start()
    pass_on(0)
    core_copy.wait_recv()

    def swap_groups(v):
        v = list(v)
        for bit in (1, 2, 4):
            low = (group // bit) % 2 == 0
            for a in range(8):
                if not a & bit:
                    lo, hi = v[a], v[a + bit]
                    v[a] = jnp.where(low, lo, pltpu.roll(hi, GROUP * bit, 1))
                    v[a + bit] = jnp.where(low, pltpu.roll(lo, LANES - GROUP * bit, 1), hi)
        return v

    for m, to in ((0, 8), (1, 16), (4, 0), (5, 24), (2, 32), (3, 40)):
        rows = swap_groups([gathered[j % 2, j // 2, m] for j in range(8)])
        for g in range(8):
            slow[(to + g) * 8 : (to + g) * 8 + 8, :] = rows[g]

    fetch_freq.wait()
    frequency = freq_ref[0]

    def coefficients(start, count, unroll):
        def body(i, carry):
            for u in range(unroll):
                r = start + i * unroll + u
                parts = node_phases(slow[at_row(r), :] * frequency)
                for which in range(2):
                    for n, value in enumerate(cosine_sums([p[which] for p in parts])):
                        H[at_row(r * 16 + which * 8 + n), :] = value
            return carry

        lax.fori_loop(0, count // unroll, body, 0)

    coefficients(1, 30, 5)
    coefficients(32, 16, 4)

    def accumulate(start, lo, count, unroll):
        def body(i, carry):
            for u in range(unroll):
                r = i * unroll + u
                total = [None] * 4
                for n in range(8):
                    hr = H[at_row((start + r) * 16 + n), :]
                    hi = H[at_row((start + r) * 16 + 8 + n), :]
                    t = [T[n, c, at_row(lo + r), :] for c in range(4)]
                    term = [
                        hr * t[0] - hi * t[1],
                        hr * t[1] + hi * t[0],
                        hr * t[2] + hi * t[3],
                        hr * t[3] - hi * t[2],
                    ]
                    total = term if n == 0 else [a + b for a, b in zip(total, term)]
                for c in range(4):
                    T[0, c, at_row(lo + r), :] = total[c]
            return carry

        lax.fori_loop(0, count // unroll, body, 0)

    def pair_copy(layer):
        return pltpu.make_async_remote_copy(
            src_ref=share.at[layer, 1 - core], dst_ref=partner_share.at[layer],
            send_sem=pair_send.at[layer], recv_sem=pair_recv.at[layer],
            device_id=partner, device_id_type=MESH,
        )

    def part_copy(layer, k):
        to = peer(k)
        return pltpu.make_async_remote_copy(
            src_ref=summed.at[layer, to % 4, :, to // 4], dst_ref=blocks.at[layer, place],
            send_sem=part_send.at[layer], recv_sem=part_recv.at[layer],
            device_id=(to * 2 + core, l), device_id_type=MESH,
        )

    def image_terms(layer):
        for m in range(2):
            terms = []
            for g in range(8):
                s_re, s_im, r_re, r_im = (T[0, c, pl.ds((TOP + 8 * m + g) * 8, 8), :] for c in range(4))
                terms.append(s_re * r_re + s_im * r_im)
            for j, value in enumerate(swap_groups(terms)):
                share[layer, j % 2, j // 2, m] = value
        pair_copy(layer).start()

    def image_parts(layer):
        pair_copy(layer).wait_recv()
        summed[layer] = share[layer, core] + partner_share[layer]
        for k in range(PEERS - 1, 0, -1):
            part_copy(layer, k).start()
        for m in range(2):
            blocks[layer, place, m : m + 1, :] = summed[layer, x, m, pl.ds(z, 1), :]

    def image_sum(layer):
        bytes_of(2 * (PEERS - 1), part_recv.at[layer]).wait()
        total = jnp.sum(blocks[layer], axis=0) * 0.125
        for m in range(2):
            row = jnp.where(diagonal, jnp.broadcast_to(total[m : m + 1, :], (8, LANES)), 0.0)
            for turn in (64, 32, 16):
                row = row + pltpu.roll(row, turn, 1)
            img_ref[layer, 8 * m : 8 * m + 8, :] = row[:, :GROUP]

    @pl.when(crossing)
    def _():
        lax.fori_loop(0, 2, first_levels, 0)

    for side in range(2):

        @pl.when(sends[side] & jnp.logical_not(middle[side]))
        def _(side=side):
            for c in range(4):
                halo_copy(c, side).wait_send()

        @pl.when(middle[side])
        def _(side=side):
            for c in range(3):
                to_relay(c, side).wait_send()
            halo_copy(3, side).wait_send()

    @pl.when((l < LAT // 2 - 1) | (l > LAT // 2))
    def _():
        from_relay(0, 0).wait_send()

    accumulate(1, TOP - 7, 30, 5)
    clear_edges()
    image_terms(0)

    levels(HALO // 2, 0)
    levels(HALO // 2, 1)
    accumulate(32, TOP, 16, 4)
    image_terms(1)
    for c in range(4):
        for t in range(2):
            for j in range(8):
                stage[c, 8 * t : 8 * t + 8, LANES * j : LANES * j + LANES] = T[
                    0, c, pl.ds((TOP + 8 * t) * 8 + j, 8, stride=8), :
                ]
    stores = [
        pltpu.make_async_copy(stage.at[pl.ds(2 * i, 2)], ref.at[0], out_sem.at[i])
        for i, ref in enumerate((src_out, rec_out))
    ]
    image_parts(1)
    image_parts(0)
    for copy in stores:
        copy.start()
    image_sum(0)
    bytes_of(4 * (PEERS - 1), own_send).wait()
    for side in range(2):

        @pl.when(sends[side])
        def _(side=side):
            bytes_of(PEERS, edge_send.at[side]).wait()

    core_copy.wait_send()
    for layer in range(2):
        pair_copy(layer).wait_send()
        bytes_of(2 * (PEERS - 1), part_send.at[layer]).wait()
    for copy in stores:
        copy.wait()
    image_sum(1)


def hand_on(*refs):
    for i in range(3):
        refs[3 + i][...] = refs[i][...]


def migrate(frequencies, slowness, src_field, rec_field):
    f32 = jnp.float32
    field = jax.ShapeDtypeStruct(src_field.shape, f32)
    dma = pltpu.SemaphoreType.DMA
    outs = pl.pallas_call(
        kernel,
        out_shape=(jax.ShapeDtypeStruct(slowness.shape, f32), field, field),
        in_specs=[
            pl.BlockSpec(memory_space=pltpu.HBM),
            pl.BlockSpec(memory_space=pltpu.HBM),
            pl.BlockSpec(memory_space=pltpu.HBM),
            pl.BlockSpec(memory_space=pltpu.HBM),
        ],
        out_specs=(
            pl.BlockSpec(memory_space=pltpu.VMEM),
            pl.BlockSpec(memory_space=pl.ANY),
            pl.BlockSpec(memory_space=pl.ANY),
        ),
        scratch_shapes=[
            pltpu.SMEM((1,), f32),
            pltpu.VMEM((2, 16, 16), f32),
            pltpu.VMEM((4, 16, 1024), f32),
            pltpu.VMEM((8, 4, ROWS * 8, LANES), f32),
            pltpu.VMEM((4, ROWS * 8, LANES), f32),
            pltpu.VMEM((48 * 16 * 8, LANES), f32),
            pltpu.VMEM((4, LANES), f32),
            pltpu.VMEM((2, 4, 6, 8, LANES), f32),
            pltpu.VMEM((48 * 8, LANES), f32),
            pltpu.VMEM((HALO * 8, LANES), f32),
            pltpu.VMEM((2, 2, 4, 2, 8, LANES), f32),
            pltpu.VMEM((2, 4, 2, 8, LANES), f32),
            pltpu.VMEM((2, 4, 2, 8, LANES), f32),
            pltpu.VMEM((2, PEERS, 2, LANES), f32),
            dma((4,)), dma((2,)),
            dma, dma,
            dma((2,)), dma((2,)),
            dma((2, 4)), dma((2, 4)),
            dma, dma,
            dma, dma,
            dma((2,)), dma((2,)),
            dma((2,)), dma((2,)),
        ],
        compiler_params=pltpu.CompilerParams(collective_id=0, has_side_effects=True, vmem_limit_bytes=64 << 20),
        name="migrate",
    )(frequencies, slowness, src_field, rec_field)
    whole = [pl.BlockSpec(memory_space=pltpu.VMEM)] * 3
    return pl.pallas_call(
        hand_on,
        out_shape=tuple(jax.ShapeDtypeStruct(out.shape, f32) for out in outs),
        in_specs=whole,
        out_specs=tuple(whole),
        name="hand_on",
    )(*outs)


def solution(mesh):
    fields = P("freq", None, "lat", None)
    return jax.shard_map(
        migrate,
        mesh=mesh,
        in_specs=(P("freq"), P(None, "lat", "freq"), fields, fields),
        out_specs=(P(None, "lat", "freq"), fields, fields),
        check_vma=False,
    )
```

```python
import math

import jax
import jax.numpy as jnp
import numpy as np
from jax import lax
from jax.experimental import pallas as pl
from jax.experimental.pallas import tpu as pltpu
from jax.sharding import PartitionSpec as P

MESH = pl.DeviceIdType.MESH
LANES, GROUP = 128, 16
ROWS, TOP, END, HALO = 48, 16, 32, 14
PEERS = 32
LAT = 8

COSINE = [0.9999983310699463, -0.499983549118042, 0.041640717536211014, -0.0013744860189035535, 2.1503588868654333e-05]
SINC = [0.9999998211860657, -0.16666515171527863, 0.008330939337611198, -0.00019708606123458594, 2.452983835610212e-06]


def polynomial(terms, t):
    value = jnp.float32(terms[-1]) * t + jnp.float32(terms[-2])
    for term in terms[-3::-1]:
        value = value * t + jnp.float32(term)
    return value


def node_phases(wavenum):
    half = 0.5 * (wavenum * wavenum)
    absorb = 0.1 * half
    absorb2 = absorb * absorb
    parts = []
    for j in range(8):
        excess = half - jnp.float32(0.5 * (math.pi * (j + 0.5) / 8) ** 2)
        square = excess * excess + absorb2
        modulus = square * lax.rsqrt(square)
        total = modulus + jnp.abs(excess)
        inverse = lax.rsqrt(total)
        larger, smaller = total * inverse, absorb * inverse
        propagating = excess >= 0
        kr = jnp.where(propagating, larger, smaller)
        ki = jnp.where(propagating, smaller, larger)
        attenuation = jnp.exp2(ki * jnp.float32(-1.4426950408889634))
        t = kr * kr
        parts.append((attenuation * polynomial(COSINE, t), (attenuation * kr) * polynomial(SINC, t)))
    return parts


def cosine_sums(p):
    def c(n, j):
        return float(np.float32((1.0 if n == 0 else 2.0) / 8 * math.cos(n * math.pi * (j + 0.5) / 8)))

    even = [p[j] + p[7 - j] for j in range(4)]
    odd = [p[j] - p[7 - j] for j in range(4)]
    s0, s1, d0, d1 = even[0] + even[3], even[1] + even[2], even[0] - even[3], even[1] - even[2]
    h = [None] * 8
    h[0] = (s0 + s1) * c(0, 0)
    h[4] = (s0 - s1) * c(4, 0)
    h[2] = d0 * c(2, 0) + d1 * c(2, 1)
    h[6] = d0 * c(6, 0) + d1 * c(6, 1)
    for n in (1, 3, 5, 7):
        h[n] = (odd[0] * c(n, 0) + odd[1] * c(n, 1)) + (odd[2] * c(n, 2) + odd[3] * c(n, 3))
    return h


def at_row(row):
    return pl.ds(pl.multiple_of(row * 8, 8), 8)


def kernel(
    freq_hbm, slow_hbm, src_ref, rec_ref, img_ref, src_out, rec_out,
    freq_ref, slow_ref, stage, T, D, H, packed, gathered, slow, relay, share, partner_share, summed, blocks,
    in_sem, out_sem, own_send, own_recv, edge_send, edge_recv, halo_send, halo_recv, relay_send, relay_recv,
    core_send, core_recv, pair_send, pair_recv, part_send, part_recv,
):
    f, l = lax.axis_index("freq"), lax.axis_index("lat")
    core, place = f % 2, f // 2
    z, x = place // 4, place % 4
    partner = (f + 1 - 2 * core, l)

    def peer(k):
        return lax.rem(place + k, PEERS)

    lane = lax.broadcasted_iota(jnp.int32, (8, LANES), 1)
    sub = lax.broadcasted_iota(jnp.int32, (8, LANES), 0)
    group = lane // GROUP
    first, last = lane == 0, lane == LANES - 1
    corner = ((sub == 0) & first) | ((sub == 7) & last)
    diagonal = sub == group

    fetches = [
        pltpu.make_async_copy(ref.at[0], stage.at[pl.ds(2 * i, 2)], in_sem.at[i])
        for i, ref in enumerate((src_ref, rec_ref))
    ]
    fetch_slow = pltpu.make_async_copy(slow_hbm, slow_ref, in_sem.at[2])
    fetch_freq = pltpu.make_async_copy(freq_hbm, freq_ref, in_sem.at[3])
    for copy in (fetch_slow, *fetches, fetch_freq):
        copy.start()

    barrier = pltpu.get_barrier_semaphore()

    def greet(device):
        pl.semaphore_signal(barrier, inc=1, device_id=device, device_id_type=MESH)

    for to in range(PEERS):

        @pl.when(to != place)
        def _(to=to):
            greet((to * 2 + core, l))

    for to in range(PEERS):

        @pl.when(l < LAT - 1)
        def _(to=to):
            greet((to * 2 + core, l + 1))

        @pl.when(l > 0)
        def _(to=to):
            greet((to * 2 + core, l - 1))

    for one, other in ((3, 0), (3, 1), (4, 0), (4, 1), (4, 2), (3, 5), (3, 6), (3, 7), (4, 6), (4, 7)):
        for here, there in ((one, other), (other, one)):

            @pl.when(l == here)
            def _(there=there):
                greet((f, there))

    greet(partner)

    fetch_slow.wait()

    for layer in range(2):
        for half in range(2):
            block = jnp.concatenate(
                [slow_ref[layer, 8 * half : 8 * half + 8, :], jnp.zeros((8, LANES - GROUP), jnp.float32)], axis=1
            )
            for turn in (16, 32, 64):
                block = block + pltpu.roll(block, turn, 1)
            row = jnp.sum(jnp.where(diagonal, block, 0.0), axis=0, keepdims=True)
            packed[2 * layer + half : 2 * layer + half + 1, :] = row

    for i, copy in enumerate(fetches):
        copy.wait()
        for c in (2 * i, 2 * i + 1):
            for t in range(2):
                for j in range(8):
                    T[0, c, pl.ds((TOP + 8 * t) * 8 + j, 8, stride=8), :] = stage[
                        c, 8 * t : 8 * t + 8, LANES * j : LANES * j + LANES
                    ]

    relays = jnp.where((l == 3) | (l == 4), 5, jnp.where((l == 2) | (l == 5), 1, 2))
    pl.semaphore_wait(barrier, PEERS + PEERS * jnp.where((l == 0) | (l == LAT - 1), 1, 2) + relays)

    def own_copy(k):
        return pltpu.make_async_remote_copy(
            src_ref=packed.at[pl.ds(0, 4)],
            dst_ref=gathered.at[core, x, pl.ds(0, 4), z],
            send_sem=own_send, recv_sem=own_recv,
            device_id=(peer(k) * 2 + core, l), device_id_type=MESH,
        )

    def edge_copy(k, side):
        return pltpu.make_async_remote_copy(
            src_ref=packed.at[1 - side],
            dst_ref=gathered.at[core, x, 4 + side, z],
            send_sem=edge_send.at[side], recv_sem=edge_recv.at[side],
            device_id=(peer(k) * 2 + core, l + 1 - 2 * side), device_id_type=MESH,
        )

    def halo_rows(side):
        down = side == 0
        return (END - HALO, TOP - HALO) if down else (TOP, END)

    def halo_copy(c, side):
        read, land = halo_rows(side)
        return pltpu.make_async_remote_copy(
            src_ref=T.at[0, c, pl.ds(read * 8, HALO * 8)],
            dst_ref=T.at[0, c, pl.ds(land * 8, HALO * 8)],
            send_sem=halo_send.at[side, c], recv_sem=halo_recv.at[side, c],
            device_id=(f, l + 1 - 2 * side), device_id_type=MESH,
        )

    def to_relay(c, side):
        read, _ = halo_rows(side)
        return pltpu.make_async_remote_copy(
            src_ref=T.at[0, c, pl.ds(read * 8, HALO * 8)], dst_ref=relay,
            send_sem=halo_send.at[side, c], recv_sem=relay_recv,
            device_id=(f, c if side == 0 else LAT - 1 - c), device_id_type=MESH,
        )

    def from_relay(c, side):
        _, land = halo_rows(side)
        return pltpu.make_async_remote_copy(
            src_ref=relay, dst_ref=T.at[0, c, pl.ds(land * 8, HALO * 8)],
            send_sem=relay_send, recv_sem=halo_recv.at[side, c],
            device_id=(f, LAT // 2 - side), device_id_type=MESH,
        )

    def bytes_of(rows, sem):
        return pltpu.make_async_copy(H.at[pl.ds(0, rows)], H.at[pl.ds(0, rows)], sem)

    sends = [l < LAT - 1, l > 0]
    receives = [l > 0, l < LAT - 1]

    middle = [l == LAT // 2 - 1, l == LAT // 2]
    crossing = middle[0] | middle[1]

    def edges_start(side):
        for k in range(PEERS - 1, -1, -1):
            edge_copy(k, side).start()

    def relays_start(side):
        for c in range(3):
            to_relay(c, side).start()
        halo_copy(3, side).start()

    @pl.when(crossing)
    def _():
        edges_start(1)

    @pl.when(middle[1])
    def _():
        relays_start(1)

    for k in range(PEERS - 1, 0, -1):
        own_copy(k).start()

    @pl.when(sends[1] & jnp.logical_not(crossing))
    def _():
        edges_start(1)

    @pl.when(sends[0])
    def _():
        edges_start(0)

    for side in (1, 0):

        @pl.when(sends[side] & jnp.logical_not(middle[side]))
        def _(side=side):
            for c in range(4):
                halo_copy(c, side).start()

    @pl.when(middle[0])
    def _():
        relays_start(0)

    for m in range(4):
        gathered[core, x, m, pl.ds(z, 1), :] = packed[m : m + 1, :]

    inside = [jnp.broadcast_to(l > 0, (1, 8, LANES)), jnp.broadcast_to(l < LAT - 1, (1, 8, LANES))]

    def clear_edges():
        for side, row in ((0, TOP - 1), (1, END)):

            @pl.when(jnp.logical_not(receives[side]))
            def _(row=row):
                for c in range(4):
                    T[0, c, pl.ds(row * 8, 8), :] = jnp.zeros((8, LANES), jnp.float32)

    clear_edges()

    def pass_on(side):
        for c in range(3):

            @pl.when(l == (c if side == 0 else LAT - 1 - c))
            def _(c=c):
                to_relay(c, side).wait_recv()
                from_relay(c, side).start()

    pass_on(1)

    def raise_rows(n, c, lo, hi, edge):
        raise_block(n, c, lo, hi - lo, edge)

    def raise_block(n, c, lo, B, edge):
        def span(row, count):
            return pl.ds(row * 8 if isinstance(row, int) else pl.multiple_of(row * 8, 8), count * 8)

        rows = span(lo, B)
        v = T[n - 1, c, span(lo - 1, B + 2), :].reshape(B + 2, 8, LANES)
        e = v[:-1] + v[1:]
        q = e[:-1] + e[1:]
        stopped = jnp.where(corner[None], 0.0, q)
        left = pltpu.roll(jnp.where(last[None], pltpu.roll(stopped, 1, 1), q), 1, 2)
        right = pltpu.roll(jnp.where(first[None], pltpu.roll(stopped, 7, 1), q), LANES - 1, 2)
        s = (left + right) + (q + q)
        d = 0.125 * s if n == 1 else 0.25 * s - D[c, rows, :].reshape(B, 8, LANES)
        D[c, rows, :] = d.reshape(B * 8, LANES)
        value = d - v[1:-1]
        if edge is not None:
            parts = [value[:-1], jnp.where(inside[0], value[-1:], 0.0)] if edge == 0 else [jnp.where(inside[1], value[:1], 0.0), value[1:]]
            value = jnp.concatenate([part for part in parts if part.shape[0]], axis=0)
        T[n, c, rows, :] = value.reshape(B * 8, LANES)

    def levels(reach, pair):
        for n in range(1, 8):
            out = reach - n
            for lo, hi, edge in ((TOP - out, TOP, 0), (TOP, TOP + 8, None), (TOP + 8, END, None), (END, END + out, 1)):
                if lo < hi:
                    for c in range(2):
                        raise_rows(n, 2 * pair + c, lo, hi, edge)

    def first_levels(pair, carry):
        for side in range(2):

            @pl.when(receives[side])
            def _(side=side):
                for c in range(2):
                    halo_copy(2 * pair + c, side).wait_recv()

        levels(HALO, pair)
        return carry

    def raise_split(pair, late):
        for n in range(1, 8):
            if late:
                lo, count = jnp.where(middle[0], END - n, TOP - HALO + n), HALO
            else:
                lo, count = jnp.where(middle[0], TOP - HALO + n, TOP + n), TOP + HALO - 2 * n
            for at in range(0, count, HALO):
                for c in range(2):
                    raise_block(n, 2 * pair + c, lo + at, min(HALO, count - at), None)

    def split_levels(late):
        def body(pair, carry):
            for m in range(2):

                @pl.when(middle[m])
                def _(m=m):
                    for c in range(2):
                        halo_copy(2 * pair + c, 1 - m if late else m).wait_recv()

            raise_split(pair, late)
            return carry

        lax.fori_loop(0, 2, body, 0)


    @pl.when(crossing)
    def _():
        split_levels(False)

    @pl.when(jnp.logical_not(crossing))
    def _():
        lax.fori_loop(0, 2, first_levels, 0)

    bytes_of(4 * (PEERS - 1), own_recv).wait()
    for side in range(2):

        @pl.when(receives[side])
        def _(side=side):
            bytes_of(PEERS, edge_recv.at[side]).wait()

    core_copy = pltpu.make_async_remote_copy(
        src_ref=gathered.at[core], dst_ref=gathered.at[core], send_sem=core_send, recv_sem=core_recv,
        device_id=partner, device_id_type=MESH,
    )
    core_copy.start()
    pass_on(0)
    core_copy.wait_recv()

    def swap_groups(v):
        v = list(v)
        for bit in (1, 2, 4):
            low = (group // bit) % 2 == 0
            for a in range(8):
                if not a & bit:
                    lo, hi = v[a], v[a + bit]
                    v[a] = jnp.where(low, lo, pltpu.roll(hi, GROUP * bit, 1))
                    v[a + bit] = jnp.where(low, pltpu.roll(lo, LANES - GROUP * bit, 1), hi)
        return v

    for m, to in ((0, 8), (1, 16), (4, 0), (5, 24), (2, 32), (3, 40)):
        rows = swap_groups([gathered[j % 2, j // 2, m] for j in range(8)])
        for g in range(8):
            slow[(to + g) * 8 : (to + g) * 8 + 8, :] = rows[g]

    fetch_freq.wait()
    frequency = freq_ref[0]

    def coefficients(start, count, unroll):
        def body(i, carry):
            for u in range(unroll):
                r = start + i * unroll + u
                parts = node_phases(slow[at_row(r), :] * frequency)
                for which in range(2):
                    for n, value in enumerate(cosine_sums([p[which] for p in parts])):
                        H[at_row(r * 16 + which * 8 + n), :] = value
            return carry

        lax.fori_loop(0, count // unroll, body, 0)

    coefficients(1, 30, 5)
    coefficients(32, 16, 4)

    def accumulate(start, lo, count, unroll):
        def body(i, carry):
            for u in range(unroll):
                r = i * unroll + u
                total = [None] * 4
                for n in range(8):
                    hr = H[at_row((start + r) * 16 + n), :]
                    hi = H[at_row((start + r) * 16 + 8 + n), :]
                    t = [T[n, c, at_row(lo + r), :] for c in range(4)]
                    term = [
                        hr * t[0] - hi * t[1],
                        hr * t[1] + hi * t[0],
                        hr * t[2] + hi * t[3],
                        hr * t[3] - hi * t[2],
                    ]
                    total = term if n == 0 else [a + b for a, b in zip(total, term)]
                for c in range(4):
                    T[0, c, at_row(lo + r), :] = total[c]
            return carry

        lax.fori_loop(0, count // unroll, body, 0)

    def pair_copy(layer):
        return pltpu.make_async_remote_copy(
            src_ref=share.at[layer, 1 - core], dst_ref=partner_share.at[layer],
            send_sem=pair_send.at[layer], recv_sem=pair_recv.at[layer],
            device_id=partner, device_id_type=MESH,
        )

    def part_copy(layer, k):
        to = peer(k)
        return pltpu.make_async_remote_copy(
            src_ref=summed.at[layer, to % 4, :, to // 4], dst_ref=blocks.at[layer, place],
            send_sem=part_send.at[layer], recv_sem=part_recv.at[layer],
            device_id=(to * 2 + core, l), device_id_type=MESH,
        )

    def image_terms(layer):
        for m in range(2):
            terms = []
            for g in range(8):
                s_re, s_im, r_re, r_im = (T[0, c, pl.ds((TOP + 8 * m + g) * 8, 8), :] for c in range(4))
                terms.append(s_re * r_re + s_im * r_im)
            for j, value in enumerate(swap_groups(terms)):
                share[layer, j % 2, j // 2, m] = value
        pair_copy(layer).start()

    def image_parts(layer):
        pair_copy(layer).wait_recv()
        summed[layer] = share[layer, core] + partner_share[layer]
        for k in range(PEERS - 1, 0, -1):
            part_copy(layer, k).start()
        for m in range(2):
            blocks[layer, place, m : m + 1, :] = summed[layer, x, m, pl.ds(z, 1), :]

    def image_sum(layer):
        bytes_of(2 * (PEERS - 1), part_recv.at[layer]).wait()
        total = jnp.sum(blocks[layer], axis=0) * 0.125
        for m in range(2):
            row = jnp.where(diagonal, jnp.broadcast_to(total[m : m + 1, :], (8, LANES)), 0.0)
            for turn in (64, 32, 16):
                row = row + pltpu.roll(row, turn, 1)
            img_ref[layer, 8 * m : 8 * m + 8, :] = row[:, :GROUP]

    @pl.when(crossing)
    def _():
        split_levels(True)

    for side in range(2):

        @pl.when(sends[side] & jnp.logical_not(middle[side]))
        def _(side=side):
            for c in range(4):
                halo_copy(c, side).wait_send()

        @pl.when(middle[side])
        def _(side=side):
            for c in range(3):
                to_relay(c, side).wait_send()
            halo_copy(3, side).wait_send()

    @pl.when((l < LAT // 2 - 1) | (l > LAT // 2))
    def _():
        from_relay(0, 0).wait_send()

    accumulate(1, TOP - 7, 30, 5)
    clear_edges()
    image_terms(0)

    levels(HALO // 2, 0)
    levels(HALO // 2, 1)
    accumulate(32, TOP, 16, 4)
    image_terms(1)
    for c in range(4):
        for t in range(2):
            for j in range(8):
                stage[c, 8 * t : 8 * t + 8, LANES * j : LANES * j + LANES] = T[
                    0, c, pl.ds((TOP + 8 * t) * 8 + j, 8, stride=8), :
                ]
    stores = [
        pltpu.make_async_copy(stage.at[pl.ds(2 * i, 2)], ref.at[0], out_sem.at[i])
        for i, ref in enumerate((src_out, rec_out))
    ]
    image_parts(1)
    image_parts(0)
    for copy in stores:
        copy.start()
    image_sum(0)
    bytes_of(4 * (PEERS - 1), own_send).wait()
    for side in range(2):

        @pl.when(sends[side])
        def _(side=side):
            bytes_of(PEERS, edge_send.at[side]).wait()

    core_copy.wait_send()
    for layer in range(2):
        pair_copy(layer).wait_send()
        bytes_of(2 * (PEERS - 1), part_send.at[layer]).wait()
    for copy in stores:
        copy.wait()
    image_sum(1)


def hand_on(*refs):
    for i in range(3):
        refs[3 + i][...] = refs[i][...]


def migrate(frequencies, slowness, src_field, rec_field):
    f32 = jnp.float32
    field = jax.ShapeDtypeStruct(src_field.shape, f32)
    dma = pltpu.SemaphoreType.DMA
    outs = pl.pallas_call(
        kernel,
        out_shape=(jax.ShapeDtypeStruct(slowness.shape, f32), field, field),
        in_specs=[
            pl.BlockSpec(memory_space=pltpu.HBM),
            pl.BlockSpec(memory_space=pltpu.HBM),
            pl.BlockSpec(memory_space=pltpu.HBM),
            pl.BlockSpec(memory_space=pltpu.HBM),
        ],
        out_specs=(
            pl.BlockSpec(memory_space=pltpu.VMEM),
            pl.BlockSpec(memory_space=pl.ANY),
            pl.BlockSpec(memory_space=pl.ANY),
        ),
        scratch_shapes=[
            pltpu.SMEM((1,), f32),
            pltpu.VMEM((2, 16, 16), f32),
            pltpu.VMEM((4, 16, 1024), f32),
            pltpu.VMEM((8, 4, ROWS * 8, LANES), f32),
            pltpu.VMEM((4, ROWS * 8, LANES), f32),
            pltpu.VMEM((48 * 16 * 8, LANES), f32),
            pltpu.VMEM((4, LANES), f32),
            pltpu.VMEM((2, 4, 6, 8, LANES), f32),
            pltpu.VMEM((48 * 8, LANES), f32),
            pltpu.VMEM((HALO * 8, LANES), f32),
            pltpu.VMEM((2, 2, 4, 2, 8, LANES), f32),
            pltpu.VMEM((2, 4, 2, 8, LANES), f32),
            pltpu.VMEM((2, 4, 2, 8, LANES), f32),
            pltpu.VMEM((2, PEERS, 2, LANES), f32),
            dma((4,)), dma((2,)),
            dma, dma,
            dma((2,)), dma((2,)),
            dma((2, 4)), dma((2, 4)),
            dma, dma,
            dma, dma,
            dma((2,)), dma((2,)),
            dma((2,)), dma((2,)),
        ],
        compiler_params=pltpu.CompilerParams(collective_id=0, has_side_effects=True, vmem_limit_bytes=64 << 20),
        name="migrate",
    )(frequencies, slowness, src_field, rec_field)
    whole = [pl.BlockSpec(memory_space=pltpu.VMEM)] * 3
    return pl.pallas_call(
        hand_on,
        out_shape=tuple(jax.ShapeDtypeStruct(out.shape, f32) for out in outs),
        in_specs=whole,
        out_specs=tuple(whole),
        name="hand_on",
    )(*outs)


def solution(mesh):
    fields = P("freq", None, "lat", None)
    return jax.shard_map(
        migrate,
        mesh=mesh,
        in_specs=(P("freq"), P(None, "lat", "freq"), fields, fields),
        out_specs=(P(None, "lat", "freq"), fields, fields),
        check_vma=False,
    )
```
